32 devices in a mesh: tm: 4 (over z), space: 8 (over y, x, core).
Axes of the slice: x: 2, y: 2, z: 4, core: 2. Of those that a mesh axis runs over, the one named last changes fastest.
Arguments:
- hindcast_archive: bfloat16 [4, 4, 16, 4, 8192], P('tm', None, None, None, 'space'), may hold values from -6 to 6
- op_blocks: bfloat16 [4, 768, 128, 128], P('tm', 'space'), may hold values from -0.5 to 0.5
- block_index: int32 [4, 768], P('tm', 'space'), may hold values from 0 to 11
- obs_values: bfloat16 [4, 4, 98304], P('tm', None, 'space'), may hold values from -6 to 6
- obs_weights: bfloat16 [4, 4, 98304], P('tm', None, 'space'), may hold values from 0.049804688 to 0.5
- obs_counts: int32 [4, 8], P('tm', 'space'), may hold values from 3072 to 12288, as said below
Outputs:
- gradient: float32 [4, 16, 4, 8192], P('tm', None, None, 'space')
The draws below stay inside these ranges and needn't reach their ends.
Inputs may be any that keep to these rules, and one draw needn't show every extreme that they name: `block_index`: A value below 2 names one of the last 2 blocks of the tile before, a value from 2 to 9 one of the tile's own blocks, a larger one the first blocks of the tile after. `obs_counts`: in every valid time some tile has all 12288 slots live; the live observations of a tile are its first slots.
All inputs are finite; a program needn't handle non-finite values.
Results may differ from the reference program's by a relative error of at most 0.0014.
Values may be sent and summed in bfloat16 or wider, within the bound.
A program may use at most 128 MiB of HBM per device.

```python
import math
import jax
import jax.numpy as jnp
from jax import lax

L = 4
ENSEMBLE_SIZE = 16
VERTICAL_LAYERS = 4
GROUP_SITE_SPAN = 128
CB_DEV = 8
OB_DEV = 96
EDGE = 2
S = 4
LEAD_STRIDE = 1
TILES = 8
NC = 8192
OBS_DEV = 12288
OBLK = 768
OBS = 98304
N_SPACE = 8


def draw_obs_counts(key, part):
    first_key, second_key = jax.random.split(jax.random.fold_in(key, 17))
    base = jax.random.randint(first_key, (S, TILES), OBS_DEV // 4, OBS_DEV + 1)
    full_tile = jax.random.randint(second_key, (S,), 0, TILES)
    tile_ids = jnp.arange(TILES, dtype=jnp.int32)[None, :]
    return jnp.where(tile_ids == full_tile[:, None], OBS_DEV, base).astype(jnp.int32)


def touch_ends(array, key, least, largest):
    extent = array.shape
    place = [jax.random.randint(jax.random.fold_in(key, axis), (), 0, extent[axis]) for axis in range(len(extent))]
    array = array.at[tuple(place)].set(least)
    longest = extent.index(max(extent))
    place[longest] = (place[longest] + 1) % extent[longest]
    return array.at[tuple(place)].set(largest)


def block_scale(own_key, shape, pieces, low, high):
    factor_of = 1.0
    for position, blocks in pieces:
        steps = jax.random.uniform(jax.random.fold_in(jax.random.fold_in(own_key, 6), position), (blocks,), jnp.float32, low / len(pieces), high / len(pieces))
        factor_of = factor_of * jnp.repeat(jnp.exp(steps), shape[position] // blocks).reshape((-1,) + (1,) * (len(shape) - 1 - position))
    return factor_of


def normal_values(own_key, extent, spread, most, shards=(), held_as=jnp.bfloat16):
    loudness = block_scale(own_key, extent, shards, -0.22, 0.18) if shards else 1.0
    values = jax.random.normal(own_key, extent, jnp.float32) * spread * loudness
    return jnp.minimum(jnp.maximum(values, -most), most).astype(held_as)


def setup_inputs(seed: int = 0) -> dict:
    key_list = jax.random.split(jax.random.key(seed), 7)
    hindcast_archive = normal_values(key_list[0], (S, L, ENSEMBLE_SIZE, VERTICAL_LAYERS, NC), 1.0, 6.0, ((0, 4), (4, 8)))
    op_blocks = normal_values(key_list[1], (S, OBLK, GROUP_SITE_SPAN, GROUP_SITE_SPAN), GROUP_SITE_SPAN ** -0.5, 0.5, ((0, 4), (1, 8)))
    block_index = touch_ends(jax.random.randint(key_list[2], (S, OBLK), 0, CB_DEV + 2 * EDGE), jax.random.fold_in(key_list[2], 1), 0, (CB_DEV + 2 * EDGE) - 1).astype(jnp.int32)
    obs_values = normal_values(key_list[3], (S, VERTICAL_LAYERS, OBS), 1.0, 6.0, ((0, 4), (2, 8)))
    obs_weights = jnp.clip(jnp.exp(math.log(0.5) - 2.306499 * jax.random.uniform(key_list[4], (S, VERTICAL_LAYERS, OBS), jnp.float32) ** block_scale(key_list[4], (S, VERTICAL_LAYERS, OBS), ((0, 4), (2, 8)), -0.2, 0.2)), 0.049804688, 0.5).astype(jnp.bfloat16)
    obs_counts = draw_obs_counts(jax.random.fold_in(key_list[6], 71), 0)
    return dict(hindcast_archive=hindcast_archive, op_blocks=op_blocks, block_index=block_index, obs_values=obs_values, obs_weights=obs_weights, obs_counts=obs_counts)


def reference(hindcast_archive, op_blocks, block_index, obs_values, obs_weights, obs_counts):
    number_of_groups = CB_DEV * N_SPACE
    owners = jnp.arange(OBLK, dtype=jnp.int32) // OB_DEV
    global_blocks = ((owners * CB_DEV)[None, :] + block_index - EDGE) % number_of_groups
    global_blocks = global_blocks.astype(jnp.int32)
    obs_index = jnp.arange(OBS, dtype=jnp.int32)
    obs_tile = obs_index // OBS_DEV
    obs_slot = obs_index % OBS_DEV
    results = []
    for launch_day in range(S):
        running = jnp.zeros((ENSEMBLE_SIZE * VERTICAL_LAYERS, number_of_groups, GROUP_SITE_SPAN), jnp.float32)
        for horizon_step in range(L):
            valid_time = (launch_day + horizon_step * LEAD_STRIDE) % S
            predicted_model_vector = hindcast_archive[launch_day, horizon_step].astype(jnp.float32).reshape(ENSEMBLE_SIZE * VERTICAL_LAYERS, number_of_groups, GROUP_SITE_SPAN)
            operator = op_blocks[valid_time].astype(jnp.float32)
            picked_matrix_lines = global_blocks[valid_time]
            collected_entries = predicted_model_vector[:, picked_matrix_lines, :]
            images = jnp.einsum("bij,cbj->cbi", operator, collected_entries).reshape(ENSEMBLE_SIZE, VERTICAL_LAYERS, OBS)
            live_mask = (obs_slot < obs_counts[valid_time][obs_tile]).astype(jnp.float32)
            misfit = ((images - obs_values[valid_time].astype(jnp.float32))
                      * obs_weights[valid_time].astype(jnp.float32) * live_mask).astype(jnp.bfloat16)
            misfit = lax.optimization_barrier(misfit)
            adjoint = jnp.einsum("bij,cbi->cbj", operator,
                                 misfit.astype(jnp.float32).reshape(ENSEMBLE_SIZE * VERTICAL_LAYERS, OBLK, GROUP_SITE_SPAN))
            summed = jax.ops.segment_sum(jnp.swapaxes(adjoint, 0, 1), picked_matrix_lines, num_segments=number_of_groups)
            running = running + jnp.swapaxes(summed, 0, 1)
        results.append(running.reshape(ENSEMBLE_SIZE, VERTICAL_LAYERS, number_of_groups * GROUP_SITE_SPAN))
    return jnp.stack(results)
```

```python
import functools

import jax
import jax.numpy as jnp
from jax import lax
from jax.experimental import pallas as pl
from jax.experimental.pallas import tpu as pltpu
from jax.sharding import PartitionSpec as P

EDGE = 2
MESH = pl.DeviceIdType.MESH
VMEM = pl.BlockSpec(memory_space=pltpu.VMEM)
ANY = pl.BlockSpec(memory_space=pl.ANY)


def neighbours(space_size, shifts, tm_size):
    me_t, me_s = lax.axis_index("tm"), lax.axis_index("space")
    left = {"space": lax.rem(me_s + space_size - 1, space_size)}
    right = {"space": lax.rem(me_s + 1, space_size)}
    ahead = [{"tm": lax.rem(me_t + shift, tm_size)} for shift in shifts]
    behind = [{"tm": lax.rem(me_t + tm_size - shift, tm_size)} for shift in shifts]
    return left, right, ahead, behind


def greet(peers):
    barrier = pltpu.get_barrier_semaphore()
    for peer in peers:
        pl.semaphore_signal(barrier, inc=1, device_id=peer, device_id_type=MESH)
    pl.semaphore_wait(barrier, len(peers))


def gather_kernel(tm_size, space_size, shifts, x_ref, ext_ref, own_sem, send_sem, recv_sem):
    leads, cells = x_ref.shape[:2]
    left, right, ahead, _ = neighbours(space_size, shifts, tm_size)
    greet([left, right, *ahead])

    def send(src, dst, lead, slot, peer):
        copy = pltpu.make_async_remote_copy(
            src_ref=src,
            dst_ref=dst,
            send_sem=send_sem.at[lead, slot],
            recv_sem=recv_sem.at[lead, slot],
            device_id=peer,
            device_id_type=MESH,
        )
        copy.start()
        return copy

    parts = ((0, EDGE), (cells - EDGE, EDGE), (EDGE, cells - 2 * EDGE))
    sent = {}
    for slot, (begin, width) in enumerate(parts):
        for lead in range(1, leads):
            sent[lead, slot] = send(
                x_ref.at[lead, pl.ds(begin, width)],
                ext_ref.at[lead, pl.ds(begin + EDGE, width)],
                lead,
                slot,
                ahead[lead - 1],
            )
    own = pltpu.make_async_copy(x_ref.at[0], ext_ref.at[0, pl.ds(EDGE, cells)], own_sem)
    own.start()
    edges = [
        send(x_ref.at[0, pl.ds(0, EDGE)], ext_ref.at[0, pl.ds(cells + EDGE, EDGE)], 0, 3, left),
        send(x_ref.at[0, pl.ds(cells - EDGE, EDGE)], ext_ref.at[0, pl.ds(0, EDGE)], 0, 4, right),
    ]
    for slot in (0, 1):
        for lead in range(1, leads):
            sent[lead, slot].wait_recv()
            if slot == 0:
                src, dst, peer = pl.ds(EDGE, EDGE), pl.ds(cells + EDGE, EDGE), left
            else:
                src, dst, peer = pl.ds(cells, EDGE), pl.ds(0, EDGE), right
            edges.append(send(ext_ref.at[lead, src], ext_ref.at[lead, dst], lead, 3 + slot, peer))
    own.wait()
    for lead in range(1, leads):
        sent[lead, 2].wait_recv()
    for copy in edges:
        copy.wait()
    for copy in sent.values():
        copy.wait_send()


def observe_kernel(index_ref, count_ref, ext_ref, op_ref, value_ref, weight_ref, out_ref):
    chunk, width = op_ref.shape[:2]
    leads, _, rows, _ = ext_ref.shape
    step = pl.program_id(0)

    @pl.when(step == 0)
    def _():
        out_ref[...] = jnp.zeros_like(out_ref)

    repeat = 8 // value_ref.shape[0]
    for k in range(chunk):
        block = step * chunk + k
        cell = index_ref[block]
        fields = ext_ref[:, cell].reshape(leads * rows, width)
        operator = op_ref[k]
        images = lax.dot_general(
            fields, operator, (((1,), (1,)), ((), ())), preferred_element_type=jnp.float32
        )
        lanes = slice(k * width, (k + 1) * width)
        observed = value_ref[:, lanes].astype(jnp.float32)
        scaling = weight_ref[:, lanes].astype(jnp.float32)
        slot = block * width + lax.broadcasted_iota(jnp.int32, scaling.shape, 1)
        scaling = jnp.where(slot < count_ref[0], scaling, 0.0)
        observed = jnp.concatenate([observed] * repeat, axis=0)
        scaling = jnp.concatenate([scaling] * repeat, axis=0)
        departures = (images.reshape(-1, 8, width) - observed[None]) * scaling[None]
        misfit = departures.reshape(leads * rows, width).astype(jnp.bfloat16)
        adjoint = jnp.dot(misfit, operator, preferred_element_type=jnp.float32)
        out_ref[:, cell] += adjoint.reshape(leads, rows, width)


def return_kernel(
    tm_size, space_size, shifts, adj_ref, out_ref, below, above, part, staged, send_sem, recv_sem
):
    leads, wide, _, width = adj_ref.shape
    cells = wide - 2 * EDGE
    left, right, _, behind = neighbours(space_size, shifts, tm_size)
    greet([left, right, *behind])

    def send(src, dst, lead, slot, peer):
        copy = pltpu.make_async_remote_copy(
            src_ref=src,
            dst_ref=dst,
            send_sem=send_sem.at[lead, slot],
            recv_sem=recv_sem.at[lead, slot],
            device_id=peer,
            device_id_type=MESH,
        )
        copy.start()
        return copy

    low, high, copies = {}, {}, []
    order = [*range(1, leads), 0]
    for lead in order:
        high[lead] = send(adj_ref.at[lead, pl.ds(0, EDGE)], above.at[lead], lead, 0, left)
        low[lead] = send(adj_ref.at[lead, pl.ds(cells + EDGE, EDGE)], below.at[lead], lead, 1, right)
    for lead in order[:-1]:
        copies.append(
            send(
                adj_ref.at[lead, pl.ds(2 * EDGE, cells - 2 * EDGE)],
                part.at[lead - 1, pl.ds(EDGE, cells - 2 * EDGE)],
                lead,
                2,
                behind[lead - 1],
            )
        )
    for lead in order[:-1]:
        low[lead].wait_recv()
        staged[lead - 1, 0] = adj_ref[lead, EDGE : 2 * EDGE] + below[lead]
        copies.append(
            send(staged.at[lead - 1, 0], part.at[lead - 1, pl.ds(0, EDGE)], lead, 3, behind[lead - 1])
        )
        high[lead].wait_recv()
        staged[lead - 1, 1] = adj_ref[lead, cells : cells + EDGE] + above[lead]
        copies.append(
            send(
                staged.at[lead - 1, 1],
                part.at[lead - 1, pl.ds(cells - EDGE, EDGE)],
                lead,
                4,
                behind[lead - 1],
            )
        )
    low[0].wait_recv()
    high[0].wait_recv()
    for copy in copies:
        copy.wait_recv()
    for cell in range(cells):
        total = adj_ref[0, cell + EDGE]
        if cell < EDGE:
            total = total + below[0, cell]
        if cell >= cells - EDGE:
            total = total + above[0, cell - (cells - EDGE)]
        for lead in range(1, leads):
            total = total + part[lead - 1, cell]
        out_ref[:, cell * width : (cell + 1) * width] = total
    for copy in (*copies, *low.values(), *high.values()):
        copy.wait_send()


def body(mesh, hindcast_archive, op_blocks, block_index, obs_values, obs_weights, obs_counts):
    tm_size, space_size = mesh.shape["tm"], mesh.shape["space"]
    _, leads, members, layers, points = hindcast_archive.shape
    _, blocks, width, _ = op_blocks.shape
    rows, cells = members * layers, points // width
    wide = cells + 2 * EDGE
    shifts = [lead * tm_size // leads for lead in range(1, leads)]
    grouped = hindcast_archive.reshape(leads, rows, cells, width).transpose(0, 2, 1, 3)
    extended = pl.pallas_call(
        functools.partial(gather_kernel, tm_size, space_size, shifts),
        out_shape=jax.ShapeDtypeStruct((leads, wide, rows, width), jnp.bfloat16),
        in_specs=[ANY],
        out_specs=ANY,
        scratch_shapes=[
            pltpu.SemaphoreType.DMA,
            pltpu.SemaphoreType.DMA((leads, 5)),
            pltpu.SemaphoreType.DMA((leads, 5)),
        ],
        compiler_params=pltpu.CompilerParams(collective_id=0, has_side_effects=True),
    )(grouped)
    chunk = 16 if blocks % 16 == 0 else 1
    adjoint = pl.pallas_call(
        observe_kernel,
        out_shape=jax.ShapeDtypeStruct((leads, wide, rows, width), jnp.float32),
        grid_spec=pltpu.PrefetchScalarGridSpec(
            num_scalar_prefetch=2,
            grid=(blocks // chunk,),
            in_specs=[
                pl.BlockSpec((leads, wide, rows, width), lambda g, *_: (0, 0, 0, 0)),
                pl.BlockSpec((chunk, width, width), lambda g, *_: (g, 0, 0)),
                pl.BlockSpec((layers, chunk * width), lambda g, *_: (0, g)),
                pl.BlockSpec((layers, chunk * width), lambda g, *_: (0, g)),
            ],
            out_specs=pl.BlockSpec((leads, wide, rows, width), lambda g, *_: (0, 0, 0, 0)),
        ),
        compiler_params=pltpu.CompilerParams(vmem_limit_bytes=32 << 20),
    )(
        block_index[0],
        obs_counts[0],
        extended,
        op_blocks[0],
        obs_values[0],
        obs_weights[0],
    )
    gradient = pl.pallas_call(
        functools.partial(return_kernel, tm_size, space_size, shifts),
        out_shape=jax.ShapeDtypeStruct((rows, points), jnp.float32),
        in_specs=[VMEM],
        out_specs=VMEM,
        scratch_shapes=[
            pltpu.VMEM((leads, EDGE, rows, width), jnp.float32),
            pltpu.VMEM((leads, EDGE, rows, width), jnp.float32),
            pltpu.VMEM((leads - 1, cells, rows, width), jnp.float32),
            pltpu.VMEM((leads - 1, 2, EDGE, rows, width), jnp.float32),
            pltpu.SemaphoreType.DMA((leads, 5)),
            pltpu.SemaphoreType.DMA((leads, 5)),
        ],
        compiler_params=pltpu.CompilerParams(
            collective_id=1, has_side_effects=True, vmem_limit_bytes=32 << 20
        ),
    )(adjoint)
    return gradient.reshape(1, members, layers, points)


def solution(mesh):
    in_specs = (
        P("tm", None, None, None, "space"),
        P("tm", "space", None, None),
        P("tm", "space"),
        P("tm", None, "space"),
        P("tm", None, "space"),
        P("tm", "space"),
    )
    out_specs = P("tm", None, None, "space")
    return jax.shard_map(
        functools.partial(body, mesh),
        mesh=mesh,
        in_specs=in_specs,
        out_specs=out_specs,
        check_vma=False,
    )
```

```python
import functools

import jax
import jax.numpy as jnp
from jax import lax
from jax.experimental import pallas as pl
from jax.experimental.pallas import tpu as pltpu
from jax.sharding import PartitionSpec as P

EDGE = 2
STEPS = 32767.0
MESH = pl.DeviceIdType.MESH
VMEM = pl.BlockSpec(memory_space=pltpu.VMEM)
ANY = pl.BlockSpec(memory_space=pl.ANY)


def neighbours(space_size, shifts, tm_size):
    me_t, me_s = lax.axis_index("tm"), lax.axis_index("space")
    left = {"space": lax.rem(me_s + space_size - 1, space_size)}
    right = {"space": lax.rem(me_s + 1, space_size)}
    ahead = [{"tm": lax.rem(me_t + shift, tm_size)} for shift in shifts]
    behind = [{"tm": lax.rem(me_t + tm_size - shift, tm_size)} for shift in shifts]
    return left, right, ahead, behind


def greet(peers):
    barrier = pltpu.get_barrier_semaphore()
    for peer in peers:
        pl.semaphore_signal(barrier, inc=1, device_id=peer, device_id_type=MESH)
    pl.semaphore_wait(barrier, len(peers))


def gather_kernel(tm_size, space_size, shifts, raw_ref, ext_ref, x_ref, own_sem, send_sem, recv_sem):
    leads, cells, rows, width = x_ref.shape

    def regroup(lead):
        for cell in range(cells):
            lanes = slice(cell * width, (cell + 1) * width)
            fields = raw_ref[lead, :, :, lanes].astype(jnp.float32)
            x_ref[lead, cell] = fields.reshape(rows, width).astype(jnp.bfloat16)

    left, right, ahead, _ = neighbours(space_size, shifts, tm_size)
    greet([left, right, *ahead])

    def send(src, dst, lead, slot, peer):
        copy = pltpu.make_async_remote_copy(
            src_ref=src,
            dst_ref=dst,
            send_sem=send_sem.at[lead, slot],
            recv_sem=recv_sem.at[lead, slot],
            device_id=peer,
            device_id_type=MESH,
        )
        copy.start()
        return copy

    parts = ((0, EDGE), (cells - EDGE, EDGE), (EDGE, cells - 2 * EDGE))
    sent = {}
    for lead in (*range(1, leads), 0):
        regroup(lead)
        for slot, (begin, count) in enumerate(parts if lead else ()):
            sent[lead, slot] = send(
                x_ref.at[lead, pl.ds(begin, count)],
                ext_ref.at[lead, pl.ds(begin + EDGE, count)],
                lead,
                slot,
                ahead[lead - 1],
            )
    own = pltpu.make_async_copy(x_ref.at[0], ext_ref.at[0, pl.ds(EDGE, cells)], own_sem)
    own.start()
    edges = [
        send(x_ref.at[0, pl.ds(0, EDGE)], ext_ref.at[0, pl.ds(cells + EDGE, EDGE)], 0, 3, left),
        send(x_ref.at[0, pl.ds(cells - EDGE, EDGE)], ext_ref.at[0, pl.ds(0, EDGE)], 0, 4, right),
    ]
    for slot in (0, 1):
        for lead in range(1, leads):
            sent[lead, slot].wait_recv()
            if slot == 0:
                src, dst, peer = pl.ds(EDGE, EDGE), pl.ds(cells + EDGE, EDGE), left
            else:
                src, dst, peer = pl.ds(cells, EDGE), pl.ds(0, EDGE), right
            edges.append(send(ext_ref.at[lead, src], ext_ref.at[lead, dst], lead, 3 + slot, peer))
    own.wait()
    for lead in range(1, leads):
        sent[lead, 2].wait_recv()
    for copy in edges:
        copy.wait()
    for copy in sent.values():
        copy.wait_send()


def observe_kernel(index_ref, count_ref, ext_ref, op_ref, value_ref, weight_ref, out_ref):
    chunk, width = op_ref.shape[:2]
    leads, _, rows, _ = ext_ref.shape
    step = pl.program_id(0)

    @pl.when(step == 0)
    def _():
        out_ref[...] = jnp.zeros_like(out_ref)

    repeat = 8 // value_ref.shape[0]
    for k in range(chunk):
        block = step * chunk + k
        cell = index_ref[block]
        fields = ext_ref[:, cell].reshape(leads * rows, width)
        operator = op_ref[k]
        images = lax.dot_general(
            fields, operator, (((1,), (1,)), ((), ())), preferred_element_type=jnp.float32
        )
        lanes = slice(k * width, (k + 1) * width)
        observed = value_ref[:, lanes].astype(jnp.float32)
        scaling = weight_ref[:, lanes].astype(jnp.float32)
        slot = block * width + lax.broadcasted_iota(jnp.int32, scaling.shape, 1)
        scaling = jnp.where(slot < count_ref[0], scaling, 0.0)
        observed = jnp.concatenate([observed] * repeat, axis=0)
        scaling = jnp.concatenate([scaling] * repeat, axis=0)
        departures = (images.reshape(-1, 8, width) - observed[None]) * scaling[None]
        misfit = departures.reshape(leads * rows, width).astype(jnp.bfloat16)
        adjoint = jnp.dot(misfit, operator, preferred_element_type=jnp.float32)
        out_ref[:, cell] += adjoint.reshape(leads, rows, width)


def encode(values, coded, scale):
    most = jnp.max(jnp.abs(values), axis=0, keepdims=True)
    most = jnp.maximum(most, 1e-30)
    coded[...] = jnp.round(values * (STEPS / most)).astype(jnp.int32).astype(jnp.int16)
    scale[...] = most * (1.0 / STEPS)


def decode(coded, scale):
    return coded.astype(jnp.int32).astype(jnp.float32) * scale


def return_kernel(
    tm_size,
    space_size,
    shifts,
    adj_ref,
    out_ref,
    below,
    above,
    own_code,
    own_scale,
    part,
    part_scale,
    send_sem,
    recv_sem,
):
    leads, wide, _, width = adj_ref.shape
    cells = wide - 2 * EDGE
    left, right, _, behind = neighbours(space_size, shifts, tm_size)
    greet([left, right, *behind])

    def send(src, dst, lead, slot, peer):
        copy = pltpu.make_async_remote_copy(
            src_ref=src,
            dst_ref=dst,
            send_sem=send_sem.at[lead, slot],
            recv_sem=recv_sem.at[lead, slot],
            device_id=peer,
            device_id_type=MESH,
        )
        copy.start()
        return copy

    low, high, copies = {}, {}, []
    order = [*range(1, leads), 0]
    for lead in order:
        high[lead] = send(adj_ref.at[lead, pl.ds(0, EDGE)], above.at[lead], lead, 0, left)
        low[lead] = send(adj_ref.at[lead, pl.ds(cells + EDGE, EDGE)], below.at[lead], lead, 1, right)

    def hand_back(lead, begin, count, slot):
        span = pl.ds(begin, count)
        for j, (own, other) in enumerate(((own_code, part), (own_scale, part_scale))):
            copies.append(
                send(
                    own.at[lead - 1, span], other.at[lead - 1, span], lead, slot + j, behind[lead - 1]
                )
            )

    for lead in order[:-1]:
        for cell in range(2 * EDGE, cells):
            encode(adj_ref[lead, cell], own_code.at[lead - 1, cell], own_scale.at[lead - 1, cell])
        hand_back(lead, 2 * EDGE, cells - 2 * EDGE, 2)
    for lead in order[:-1]:
        low[lead].wait_recv()
        high[lead].wait_recv()
        for e in range(EDGE):
            encode(
                adj_ref[lead, EDGE + e] + below[lead, e],
                own_code.at[lead - 1, e],
                own_scale.at[lead - 1, e],
            )
            encode(
                adj_ref[lead, cells + e] + above[lead, e],
                own_code.at[lead - 1, EDGE + e],
                own_scale.at[lead - 1, EDGE + e],
            )
        hand_back(lead, 0, 2 * EDGE, 4)
    low[0].wait_recv()
    high[0].wait_recv()
    for copy in copies:
        copy.wait_recv()
    for cell in range(cells):
        total = adj_ref[0, cell + EDGE]
        place = cell + EDGE
        if cell < EDGE:
            total = total + below[0, cell]
            place = cell
        if cell >= cells - EDGE:
            total = total + above[0, cell - (cells - EDGE)]
            place = cell - (cells - EDGE) + EDGE
        for lead in range(1, leads):
            total = total + decode(part[lead - 1, place], part_scale[lead - 1, place])
        out_ref[:, cell * width : (cell + 1) * width] = total
    for copy in (*copies, *low.values(), *high.values()):
        copy.wait_send()


def body(mesh, hindcast_archive, op_blocks, block_index, obs_values, obs_weights, obs_counts):
    tm_size, space_size = mesh.shape["tm"], mesh.shape["space"]
    _, leads, members, layers, points = hindcast_archive.shape
    _, blocks, width, _ = op_blocks.shape
    rows, cells = members * layers, points // width
    wide = cells + 2 * EDGE
    shifts = [lead * tm_size // leads for lead in range(1, leads)]
    extended = pl.pallas_call(
        functools.partial(gather_kernel, tm_size, space_size, shifts),
        out_shape=jax.ShapeDtypeStruct((leads, wide, rows, width), jnp.bfloat16),
        in_specs=[VMEM],
        out_specs=ANY,
        scratch_shapes=[
            pltpu.VMEM((leads, cells, rows, width), jnp.bfloat16),
            pltpu.SemaphoreType.DMA,
            pltpu.SemaphoreType.DMA((leads, 5)),
            pltpu.SemaphoreType.DMA((leads, 5)),
        ],
        compiler_params=pltpu.CompilerParams(collective_id=0, has_side_effects=True),
    )(hindcast_archive[0])
    chunk = 16 if blocks % 16 == 0 else 1
    adjoint = pl.pallas_call(
        observe_kernel,
        out_shape=jax.ShapeDtypeStruct((leads, wide, rows, width), jnp.float32),
        grid_spec=pltpu.PrefetchScalarGridSpec(
            num_scalar_prefetch=2,
            grid=(blocks // chunk,),
            in_specs=[
                pl.BlockSpec((leads, wide, rows, width), lambda g, *_: (0, 0, 0, 0)),
                pl.BlockSpec((chunk, width, width), lambda g, *_: (g, 0, 0)),
                pl.BlockSpec((layers, chunk * width), lambda g, *_: (0, g)),
                pl.BlockSpec((layers, chunk * width), lambda g, *_: (0, g)),
            ],
            out_specs=pl.BlockSpec((leads, wide, rows, width), lambda g, *_: (0, 0, 0, 0)),
        ),
        compiler_params=pltpu.CompilerParams(vmem_limit_bytes=32 << 20),
    )(
        block_index[0],
        obs_counts[0],
        extended,
        op_blocks[0],
        obs_values[0],
        obs_weights[0],
    )
    gradient = pl.pallas_call(
        functools.partial(return_kernel, tm_size, space_size, shifts),
        out_shape=jax.ShapeDtypeStruct((rows, points), jnp.float32),
        in_specs=[VMEM],
        out_specs=VMEM,
        scratch_shapes=[
            pltpu.VMEM((leads, EDGE, rows, width), jnp.float32),
            pltpu.VMEM((leads, EDGE, rows, width), jnp.float32),
            pltpu.VMEM((leads - 1, cells, rows, width), jnp.int16),
            pltpu.VMEM((leads - 1, cells, 1, width), jnp.float32),
            pltpu.VMEM((leads - 1, cells, rows, width), jnp.int16),
            pltpu.VMEM((leads - 1, cells, 1, width), jnp.float32),
            pltpu.SemaphoreType.DMA((leads, 6)),
            pltpu.SemaphoreType.DMA((leads, 6)),
        ],
        compiler_params=pltpu.CompilerParams(
            collective_id=1, has_side_effects=True, vmem_limit_bytes=32 << 20
        ),
    )(adjoint)
    return gradient.reshape(1, members, layers, points)


def solution(mesh):
    in_specs = (
        P("tm", None, None, None, "space"),
        P("tm", "space", None, None),
        P("tm", "space"),
        P("tm", None, "space"),
        P("tm", None, "space"),
        P("tm", "space"),
    )
    out_specs = P("tm", None, None, "space")
    return jax.shard_map(
        functools.partial(body, mesh),
        mesh=mesh,
        in_specs=in_specs,
        out_specs=out_specs,
        check_vma=False,
    )
```

```python
import functools

import jax
import jax.numpy as jnp
from jax import lax
from jax.experimental import pallas as pl
from jax.experimental.pallas import tpu as pltpu
from jax.sharding import PartitionSpec as P

EDGE = 2
PARTS = 2
CHUNK = 8
STEPS = 32767.0
MESH = pl.DeviceIdType.MESH
VMEM = pl.BlockSpec(memory_space=pltpu.VMEM)
HBM = pl.BlockSpec(memory_space=pltpu.HBM)


def neighbours(space_size, shifts, tm_size):
    me_t, me_s = lax.axis_index("tm"), lax.axis_index("space")
    left = {"space": lax.rem(me_s + space_size - 1, space_size)}
    right = {"space": lax.rem(me_s + 1, space_size)}
    ahead = [{"tm": lax.rem(me_t + shift, tm_size)} for shift in shifts]
    behind = [{"tm": lax.rem(me_t + tm_size - shift, tm_size)} for shift in shifts]
    return left, right, ahead, behind


def greet(peers):
    barrier = pltpu.get_barrier_semaphore()
    for peer in peers:
        pl.semaphore_signal(barrier, inc=1, device_id=peer, device_id_type=MESH)
    pl.semaphore_wait(barrier, len(peers))


def encode(values, coded, scale):
    most = jnp.max(jnp.abs(values), axis=0, keepdims=True)
    most = jnp.maximum(most, 1e-30)
    coded[...] = jnp.round(values * (STEPS / most)).astype(jnp.int32).astype(jnp.int16)
    scale[...] = most * (1.0 / STEPS)


def decode(coded, scale):
    return coded.astype(jnp.int32).astype(jnp.float32) * scale


def fused_kernel(
    tm_size,
    space_size,
    shifts,
    parts,
    index_ref,
    prev_ref,
    last_ref,
    count_ref,
    raw_hbm,
    op_hbm,
    value_hbm,
    weight_hbm,
    out_ref,
    raw_ref,
    op_ref,
    value_ref,
    weight_ref,
    x_ref,
    sums,
    adj,
    above,
    below,
    own_code,
    own_scale,
    part,
    part_scale,
    load_sem,
    go_send,
    go_recv,
    back_send,
    back_recv,
    *extended,
):
    _, leads, cells, rows, width = x_ref.shape
    blocks = op_ref.shape[0]
    members = raw_ref.shape[1] // parts
    wide = cells + 2 * EDGE
    left, right, ahead, behind = neighbours(space_size, shifts, tm_size)

    order = [*range(1, leads), 0]
    raw_loads = {
        lead: pltpu.make_async_copy(raw_hbm.at[lead], raw_ref.at[lead], load_sem.at[3 + lead])
        for lead in order
    }
    loads = [
        pltpu.make_async_copy(op_hbm, op_ref, load_sem.at[0]),
        pltpu.make_async_copy(value_hbm, value_ref, load_sem.at[1]),
        pltpu.make_async_copy(weight_hbm, weight_ref, load_sem.at[2]),
    ]
    for load in (*raw_loads.values(), *loads):
        load.start()
    sums[blocks] = jnp.zeros(sums.shape[1:], sums.dtype)
    greet([left, right, *ahead])

    def sender(send_sem, recv_sem):
        def send(src, dst, place, peer):
            copy = pltpu.make_async_remote_copy(
                src_ref=src,
                dst_ref=dst,
                send_sem=send_sem.at[place],
                recv_sem=recv_sem.at[place],
                device_id=peer,
                device_id_type=MESH,
            )
            copy.start()
            return copy

        return send

    go, back = sender(go_send, go_recv), sender(back_send, back_recv)
    pieces = ((0, EDGE), (cells - EDGE, EDGE), (EDGE, cells - 2 * EDGE))
    sent, edges = {}, {}
    for h in range(parts):
        for lead in order:
            if h == 0:
                raw_loads[lead].wait()
            for cell in range(cells):
                lanes = slice(cell * width, (cell + 1) * width)
                fields = raw_ref[lead, h * members : (h + 1) * members, :, lanes].astype(jnp.float32)
                fields = fields.reshape(rows, width).astype(jnp.bfloat16)
                x_ref[h, lead, cell] = fields
                if lead == 0:
                    extended[h][0, cell + EDGE] = fields
            for slot, (begin, span) in enumerate(pieces if lead else ()):
                sent[h, lead, slot] = go(
                    x_ref.at[h, lead, pl.ds(begin, span)],
                    extended[h].at[lead, pl.ds(begin + EDGE, span)],
                    (h, lead, slot),
                    ahead[lead - 1],
                )
        edges[h, 0, 0] = go(
            x_ref.at[h, 0, pl.ds(0, EDGE)],
            extended[h].at[0, pl.ds(cells + EDGE, EDGE)],
            (h, 0, 3),
            left,
        )
        edges[h, 0, 1] = go(
            x_ref.at[h, 0, pl.ds(cells - EDGE, EDGE)],
            extended[h].at[0, pl.ds(0, EDGE)],
            (h, 0, 4),
            right,
        )

    def forward_edges(h):
        for lead in range(1, leads):
            for slot in (0, 1):
                sent[h, lead, slot].wait_recv()
                if slot == 0:
                    src, dst, peer = pl.ds(EDGE, EDGE), pl.ds(cells + EDGE, EDGE), left
                else:
                    src, dst, peer = pl.ds(cells, EDGE), pl.ds(0, EDGE), right
                edges[h, lead, slot] = go(
                    extended[h].at[lead, src], extended[h].at[lead, dst], (h, lead, 3 + slot), peer
                )

    def await_fields(h):
        for lead in range(1, leads):
            sent[h, lead, 2].wait_recv()
        for lead in range(leads):
            for slot in (0, 1):
                edges[h, lead, slot].wait_recv()

    repeat = 8 // value_ref.shape[0]

    def observe(h, begin, end):
        def chunk(step, carry):
            for k in range(CHUNK):
                block = step * CHUNK + k
                operator = op_ref[block]
                fields = extended[h][:, index_ref[block]].reshape(leads * rows, width)
                images = lax.dot_general(
                    fields, operator, (((1,), (1,)), ((), ())), preferred_element_type=jnp.float32
                )
                lanes = pl.ds(pl.multiple_of(block * width, width), width)
                observed = value_ref[:, lanes].astype(jnp.float32)
                scaling = weight_ref[:, lanes].astype(jnp.float32)
                slot = block * width + lax.broadcasted_iota(jnp.int32, scaling.shape, 1)
                scaling = jnp.where(slot < count_ref[0], scaling, 0.0)
                observed = jnp.concatenate([observed] * repeat, axis=0)
                scaling = jnp.concatenate([scaling] * repeat, axis=0)
                departures = (images.reshape(-1, 8, width) - observed[None]) * scaling[None]
                misfit = departures.reshape(leads * rows, width).astype(jnp.bfloat16)
                adjoint = jnp.dot(misfit, operator, preferred_element_type=jnp.float32)
                sums[block] = adjoint + sums[prev_ref[block]]
            return carry

        lax.fori_loop(begin // CHUNK, end // CHUNK, chunk, 0)

    low, high, copies = {}, {}, []

    def hand_back(h, lead, begin, span, slot):
        span = pl.ds(begin, span)
        for j, (own, other) in enumerate(((own_code, part), (own_scale, part_scale))):
            copies.append(
                back(
                    own.at[h, lead - 1, span],
                    other.at[h, lead - 1, span],
                    (h, lead, slot + j),
                    behind[lead - 1],
                )
            )

    def put(h, lead, place, values):
        encode(values, own_code.at[h, lead - 1, place], own_scale.at[h, lead - 1, place])

    def return_middle(h):
        for cell in (*range(EDGE), *range(cells + EDGE, wide), *range(EDGE, cells + EDGE)):
            adj[h, :, cell] = sums[last_ref[cell]].reshape(leads, rows, width)
        for lead in order:
            high[h, lead] = back(adj.at[h, lead, pl.ds(0, EDGE)], above.at[h, lead], (h, lead, 0), left)
            low[h, lead] = back(
                adj.at[h, lead, pl.ds(cells + EDGE, EDGE)], below.at[h, lead], (h, lead, 1), right
            )
        for lead in order[:-1]:
            for cell in range(2 * EDGE, cells):
                put(h, lead, cell, adj[h, lead, cell])
            hand_back(h, lead, 2 * EDGE, cells - 2 * EDGE, 2)

    def return_edges(h):
        for lead in order[:-1]:
            low[h, lead].wait_recv()
            high[h, lead].wait_recv()
            for e in range(EDGE):
                put(h, lead, e, adj[h, lead, EDGE + e] + below[h, lead, e])
                put(h, lead, EDGE + e, adj[h, lead, cells + e] + above[h, lead, e])
            hand_back(h, lead, 0, 2 * EDGE, 4)

    middle = blocks // 2 // CHUNK * CHUNK
    forward_edges(0)
    for load in loads:
        load.wait()
    for h in range(parts):
        await_fields(h)
        observe(h, 0, middle)
        if h + 1 < parts:
            forward_edges(h + 1)
        if h:
            return_edges(h - 1)
        observe(h, middle, blocks)
        return_middle(h)
    return_edges(parts - 1)
    for h in range(parts):
        low[h, 0].wait_recv()
        high[h, 0].wait_recv()
    for copy in copies:
        copy.wait_recv()
    for h in range(parts):
        for cell in range(cells):
            total = adj[h, 0, cell + EDGE]
            place = cell + EDGE
            if cell < EDGE:
                total = total + below[h, 0, cell]
                place = cell
            if cell >= cells - EDGE:
                total = total + above[h, 0, cell - (cells - EDGE)]
                place = cell - (cells - EDGE) + EDGE
            for lead in range(1, leads):
                total = total + decode(part[h, lead - 1, place], part_scale[h, lead - 1, place])
            out_ref[h * rows : (h + 1) * rows, cell * width : (cell + 1) * width] = total
    for copy in (*copies, *low.values(), *high.values(), *sent.values(), *edges.values()):
        copy.wait_send()


def links(index, wide):
    blocks = index.shape[0]
    order = lax.broadcasted_iota(jnp.int32, (blocks, blocks), 1)
    own = lax.broadcasted_iota(jnp.int32, (blocks, blocks), 0)
    same = (index[None, :] == index[:, None]) & (order < own)
    prev = jnp.max(jnp.where(same, order, -1), axis=1)
    cell = lax.broadcasted_iota(jnp.int32, (wide, blocks), 0)
    last = jnp.max(jnp.where(index[None, :] == cell, order[:wide], -1), axis=1)
    return jnp.where(prev < 0, blocks, prev), jnp.where(last < 0, blocks, last)


def body(mesh, hindcast_archive, op_blocks, block_index, obs_values, obs_weights, obs_counts):
    tm_size, space_size = mesh.shape["tm"], mesh.shape["space"]
    _, leads, members, layers, points = hindcast_archive.shape
    _, blocks, width, _ = op_blocks.shape
    cells = points // width
    rows = members * layers // PARTS
    wide = cells + 2 * EDGE
    shifts = [lead * tm_size // leads for lead in range(1, leads)]
    prev, last = links(block_index[0], wide)
    smem = pl.BlockSpec(memory_space=pltpu.SMEM)
    gradient = pl.pallas_call(
        functools.partial(fused_kernel, tm_size, space_size, shifts, PARTS),
        out_shape=jax.ShapeDtypeStruct((members * layers, points), jnp.float32),
        in_specs=[smem] * 4 + [HBM] * 4,
        out_specs=VMEM,
        scratch_shapes=[
            pltpu.VMEM(hindcast_archive.shape[1:], jnp.bfloat16),
            pltpu.VMEM(op_blocks.shape[1:], jnp.bfloat16),
            pltpu.VMEM(obs_values.shape[1:], jnp.bfloat16),
            pltpu.VMEM(obs_weights.shape[1:], jnp.bfloat16),
            pltpu.VMEM((PARTS, leads, cells, rows, width), jnp.bfloat16),
            pltpu.VMEM((blocks + 1, leads * rows, width), jnp.float32),
            pltpu.VMEM((PARTS, leads, wide, rows, width), jnp.float32),
            pltpu.VMEM((PARTS, leads, EDGE, rows, width), jnp.float32),
            pltpu.VMEM((PARTS, leads, EDGE, rows, width), jnp.float32),
            pltpu.VMEM((PARTS, leads - 1, cells, rows, width), jnp.int16),
            pltpu.VMEM((PARTS, leads - 1, cells, 1, width), jnp.float32),
            pltpu.VMEM((PARTS, leads - 1, cells, rows, width), jnp.int16),
            pltpu.VMEM((PARTS, leads - 1, cells, 1, width), jnp.float32),
            pltpu.SemaphoreType.DMA((3 + leads,)),
            pltpu.SemaphoreType.DMA((PARTS, leads, 5)),
            pltpu.SemaphoreType.DMA((PARTS, leads, 5)),
            pltpu.SemaphoreType.DMA((PARTS, leads, 6)),
            pltpu.SemaphoreType.DMA((PARTS, leads, 6)),
        ]
        + [pltpu.VMEM((leads, wide, rows, width), jnp.bfloat16)] * PARTS,
        compiler_params=pltpu.CompilerParams(
            collective_id=0, has_side_effects=True, vmem_limit_bytes=48 << 20
        ),
    )(
        block_index[0],
        prev,
        last,
        obs_counts[0],
        hindcast_archive[0],
        op_blocks[0],
        obs_values[0],
        obs_weights[0],
    )
    return gradient.reshape(1, members, layers, points)


def solution(mesh):
    in_specs = (
        P("tm", None, None, None, "space"),
        P("tm", "space", None, None),
        P("tm", "space"),
        P("tm", None, "space"),
        P("tm", None, "space"),
        P("tm", "space"),
    )
    out_specs = P("tm", None, None, "space")
    return jax.shard_map(
        functools.partial(body, mesh),
        mesh=mesh,
        in_specs=in_specs,
        out_specs=out_specs,
        check_vma=False,
    )
```

```python
import functools

import jax
import jax.numpy as jnp
from jax import lax
from jax.experimental import pallas as pl
from jax.experimental.pallas import tpu as pltpu
from jax.sharding import PartitionSpec as P

EDGE = 2
STEPS = 32767.0
MESH = pl.DeviceIdType.MESH
VMEM = pl.BlockSpec(memory_space=pltpu.VMEM)
ANY = pl.BlockSpec(memory_space=pl.ANY)


def neighbours(space_size, shifts, tm_size):
    me_t, me_s = lax.axis_index("tm"), lax.axis_index("space")
    left = {"space": lax.rem(me_s + space_size - 1, space_size)}
    right = {"space": lax.rem(me_s + 1, space_size)}
    ahead = [{"tm": lax.rem(me_t + shift, tm_size)} for shift in shifts]
    behind = [{"tm": lax.rem(me_t + tm_size - shift, tm_size)} for shift in shifts]
    return left, right, ahead, behind


def greet(peers):
    barrier = pltpu.get_barrier_semaphore()
    for peer in peers:
        pl.semaphore_signal(barrier, inc=1, device_id=peer, device_id_type=MESH)
    pl.semaphore_wait(barrier, len(peers))


def gather_kernel(tm_size, space_size, shifts, raw_ref, ext_ref, x_ref, own_sem, send_sem, recv_sem):
    leads, cells, rows, width = x_ref.shape

    def regroup(lead):
        for cell in range(cells):
            lanes = slice(cell * width, (cell + 1) * width)
            fields = raw_ref[lead, :, :, lanes].astype(jnp.float32)
            x_ref[lead, cell] = fields.reshape(rows, width).astype(jnp.bfloat16)

    left, right, ahead, _ = neighbours(space_size, shifts, tm_size)
    greet([left, right, *ahead])

    def send(src, dst, lead, slot, peer):
        copy = pltpu.make_async_remote_copy(
            src_ref=src,
            dst_ref=dst,
            send_sem=send_sem.at[lead, slot],
            recv_sem=recv_sem.at[lead, slot],
            device_id=peer,
            device_id_type=MESH,
        )
        copy.start()
        return copy

    parts = ((0, EDGE), (cells - EDGE, EDGE), (EDGE, cells - 2 * EDGE))
    sent = {}
    for lead in (*range(1, leads), 0):
        regroup(lead)
        for slot, (begin, count) in enumerate(parts if lead else ()):
            sent[lead, slot] = send(
                x_ref.at[lead, pl.ds(begin, count)],
                ext_ref.at[lead, pl.ds(begin + EDGE, count)],
                lead,
                slot,
                ahead[lead - 1],
            )
    own = pltpu.make_async_copy(x_ref.at[0], ext_ref.at[0, pl.ds(EDGE, cells)], own_sem)
    own.start()
    edges = [
        send(x_ref.at[0, pl.ds(0, EDGE)], ext_ref.at[0, pl.ds(cells + EDGE, EDGE)], 0, 3, left),
        send(x_ref.at[0, pl.ds(cells - EDGE, EDGE)], ext_ref.at[0, pl.ds(0, EDGE)], 0, 4, right),
    ]
    for slot in (0, 1):
        for lead in range(1, leads):
            sent[lead, slot].wait_recv()
            if slot == 0:
                src, dst, peer = pl.ds(EDGE, EDGE), pl.ds(cells + EDGE, EDGE), left
            else:
                src, dst, peer = pl.ds(cells, EDGE), pl.ds(0, EDGE), right
            edges.append(send(ext_ref.at[lead, src], ext_ref.at[lead, dst], lead, 3 + slot, peer))
    own.wait()
    for lead in range(1, leads):
        sent[lead, 2].wait_recv()
    for copy in edges:
        copy.wait()
    for copy in sent.values():
        copy.wait_send()


def observe_kernel(index_ref, count_ref, ext_ref, op_ref, value_ref, weight_ref, out_ref):
    chunk, width = op_ref.shape[:2]
    leads, _, rows, _ = ext_ref.shape
    step = pl.program_id(0)

    @pl.when(step == 0)
    def _():
        out_ref[...] = jnp.zeros_like(out_ref)

    repeat = 8 // value_ref.shape[0]
    for k in range(chunk):
        block = step * chunk + k
        cell = index_ref[block]
        fields = ext_ref[:, cell].reshape(leads * rows, width)
        operator = op_ref[k]
        images = lax.dot_general(
            fields, operator, (((1,), (1,)), ((), ())), preferred_element_type=jnp.float32
        )
        lanes = slice(k * width, (k + 1) * width)
        observed = value_ref[:, lanes].astype(jnp.float32)
        scaling = weight_ref[:, lanes].astype(jnp.float32)
        slot = block * width + lax.broadcasted_iota(jnp.int32, scaling.shape, 1)
        scaling = jnp.where(slot < count_ref[0], scaling, 0.0)
        observed = jnp.concatenate([observed] * repeat, axis=0)
        scaling = jnp.concatenate([scaling] * repeat, axis=0)
        departures = (images.reshape(-1, 8, width) - observed[None]) * scaling[None]
        misfit = departures.reshape(leads * rows, width).astype(jnp.bfloat16)
        adjoint = jnp.dot(misfit, operator, preferred_element_type=jnp.float32)
        out_ref[:, cell] += adjoint.reshape(leads, rows, width)


def encode(values, coded, scale):
    most = jnp.max(jnp.abs(values), axis=0, keepdims=True)
    most = jnp.maximum(most, 1e-30)
    coded[...] = jnp.round(values * (STEPS / most)).astype(jnp.int32).astype(jnp.int16)
    scale[...] = most * (1.0 / STEPS)


def decode(coded, scale):
    return coded.astype(jnp.int32).astype(jnp.float32) * scale


def return_kernel(
    tm_size,
    space_size,
    shifts,
    adj_ref,
    out_ref,
    below,
    above,
    own_code,
    own_scale,
    part,
    part_scale,
    send_sem,
    recv_sem,
):
    leads, wide, _, width = adj_ref.shape
    cells = wide - 2 * EDGE
    left, right, _, behind = neighbours(space_size, shifts, tm_size)
    greet([left, right, *behind])

    def send(src, dst, lead, slot, peer):
        copy = pltpu.make_async_remote_copy(
            src_ref=src,
            dst_ref=dst,
            send_sem=send_sem.at[lead, slot],
            recv_sem=recv_sem.at[lead, slot],
            device_id=peer,
            device_id_type=MESH,
        )
        copy.start()
        return copy

    low, high, copies = {}, {}, []
    order = [*range(1, leads), 0]
    for lead in order:
        high[lead] = send(adj_ref.at[lead, pl.ds(0, EDGE)], above.at[lead], lead, 0, left)
        low[lead] = send(adj_ref.at[lead, pl.ds(cells + EDGE, EDGE)], below.at[lead], lead, 1, right)

    def hand_back(lead, begin, count, slot):
        span = pl.ds(begin, count)
        for j, (own, other) in enumerate(((own_code, part), (own_scale, part_scale))):
            copies.append(
                send(
                    own.at[lead - 1, span], other.at[lead - 1, span], lead, slot + j, behind[lead - 1]
                )
            )

    for lead in order[:-1]:
        for cell in range(2 * EDGE, cells):
            encode(adj_ref[lead, cell], own_code.at[lead - 1, cell], own_scale.at[lead - 1, cell])
        hand_back(lead, 2 * EDGE, cells - 2 * EDGE, 2)
    for lead in order[:-1]:
        low[lead].wait_recv()
        high[lead].wait_recv()
        for e in range(EDGE):
            encode(
                adj_ref[lead, EDGE + e] + below[lead, e],
                own_code.at[lead - 1, e],
                own_scale.at[lead - 1, e],
            )
            encode(
                adj_ref[lead, cells + e] + above[lead, e],
                own_code.at[lead - 1, EDGE + e],
                own_scale.at[lead - 1, EDGE + e],
            )
        hand_back(lead, 0, 2 * EDGE, 4)
    low[0].wait_recv()
    high[0].wait_recv()
    for copy in copies:
        copy.wait_recv()
    for cell in range(cells):
        total = adj_ref[0, cell + EDGE]
        place = cell + EDGE
        if cell < EDGE:
            total = total + below[0, cell]
            place = cell
        if cell >= cells - EDGE:
            total = total + above[0, cell - (cells - EDGE)]
            place = cell - (cells - EDGE) + EDGE
        for lead in range(1, leads):
            total = total + decode(part[lead - 1, place], part_scale[lead - 1, place])
        out_ref[:, cell * width : (cell + 1) * width] = total
    for copy in (*copies, *low.values(), *high.values()):
        copy.wait_send()


def body(mesh, hindcast_archive, op_blocks, block_index, obs_values, obs_weights, obs_counts):
    tm_size, space_size = mesh.shape["tm"], mesh.shape["space"]
    _, leads, members, layers, points = hindcast_archive.shape
    _, blocks, width, _ = op_blocks.shape
    rows, cells = members * layers, points // width
    wide = cells + 2 * EDGE
    shifts = [lead * tm_size // leads for lead in range(1, leads)]
    extended = pl.pallas_call(
        functools.partial(gather_kernel, tm_size, space_size, shifts),
        out_shape=jax.ShapeDtypeStruct((leads, wide, rows, width), jnp.bfloat16),
        in_specs=[VMEM],
        out_specs=ANY,
        scratch_shapes=[
            pltpu.VMEM((leads, cells, rows, width), jnp.bfloat16),
            pltpu.SemaphoreType.DMA,
            pltpu.SemaphoreType.DMA((leads, 5)),
            pltpu.SemaphoreType.DMA((leads, 5)),
        ],
        compiler_params=pltpu.CompilerParams(collective_id=0, has_side_effects=True),
    )(hindcast_archive[0])
    chunk = 16 if blocks % 16 == 0 else 1
    adjoint = pl.pallas_call(
        observe_kernel,
        out_shape=jax.ShapeDtypeStruct((leads, wide, rows, width), jnp.float32),
        grid_spec=pltpu.PrefetchScalarGridSpec(
            num_scalar_prefetch=2,
            grid=(blocks // chunk,),
            in_specs=[
                pl.BlockSpec((leads, wide, rows, width), lambda g, *_: (0, 0, 0, 0)),
                pl.BlockSpec((chunk, width, width), lambda g, *_: (g, 0, 0)),
                pl.BlockSpec((layers, chunk * width), lambda g, *_: (0, g)),
                pl.BlockSpec((layers, chunk * width), lambda g, *_: (0, g)),
            ],
            out_specs=pl.BlockSpec((leads, wide, rows, width), lambda g, *_: (0, 0, 0, 0)),
        ),
        compiler_params=pltpu.CompilerParams(vmem_limit_bytes=63 << 20),
    )(
        block_index[0],
        obs_counts[0],
        extended,
        op_blocks[0],
        obs_values[0],
        obs_weights[0],
    )
    gradient = pl.pallas_call(
        functools.partial(return_kernel, tm_size, space_size, shifts),
        out_shape=jax.ShapeDtypeStruct((rows, points), jnp.float32),
        in_specs=[VMEM],
        out_specs=VMEM,
        scratch_shapes=[
            pltpu.VMEM((leads, EDGE, rows, width), jnp.float32),
            pltpu.VMEM((leads, EDGE, rows, width), jnp.float32),
            pltpu.VMEM((leads - 1, cells, rows, width), jnp.int16),
            pltpu.VMEM((leads - 1, cells, 1, width), jnp.float32),
            pltpu.VMEM((leads - 1, cells, rows, width), jnp.int16),
            pltpu.VMEM((leads - 1, cells, 1, width), jnp.float32),
            pltpu.SemaphoreType.DMA((leads, 6)),
            pltpu.SemaphoreType.DMA((leads, 6)),
        ],
        compiler_params=pltpu.CompilerParams(
            collective_id=1, has_side_effects=True, vmem_limit_bytes=32 << 20
        ),
    )(adjoint)
    return gradient.reshape(1, members, layers, points)


def solution(mesh):
    in_specs = (
        P("tm", None, None, None, "space"),
        P("tm", "space", None, None),
        P("tm", "space"),
        P("tm", None, "space"),
        P("tm", None, "space"),
        P("tm", "space"),
    )
    out_specs = P("tm", None, None, "space")
    return jax.shard_map(
        functools.partial(body, mesh),
        mesh=mesh,
        in_specs=in_specs,
        out_specs=out_specs,
        check_vma=False,
    )
```

```python
import functools

import jax
import jax.numpy as jnp
from jax import lax
from jax.experimental import pallas as pl
from jax.experimental.pallas import tpu as pltpu
from jax.sharding import PartitionSpec as P

EDGE = 2
STEPS = 32767.0
MESH = pl.DeviceIdType.MESH
VMEM = pl.BlockSpec(memory_space=pltpu.VMEM)
ANY = pl.BlockSpec(memory_space=pl.ANY)


def neighbours(space_size, shifts, tm_size):
    me_t, me_s = lax.axis_index("tm"), lax.axis_index("space")
    left = {"space": lax.rem(me_s + space_size - 1, space_size)}
    right = {"space": lax.rem(me_s + 1, space_size)}
    ahead = [{"tm": lax.rem(me_t + shift, tm_size)} for shift in shifts]
    behind = [{"tm": lax.rem(me_t + tm_size - shift, tm_size)} for shift in shifts]
    return left, right, ahead, behind


def greet(peers):
    barrier = pltpu.get_barrier_semaphore()
    for peer in peers:
        pl.semaphore_signal(barrier, inc=1, device_id=peer, device_id_type=MESH)
    pl.semaphore_wait(barrier, len(peers))


def gather_kernel(tm_size, space_size, shifts, raw_ref, ext_ref, x_ref, own_sem, send_sem, recv_sem):
    leads, cells, rows, width = x_ref.shape

    def regroup(lead):
        for cell in range(cells):
            lanes = slice(cell * width, (cell + 1) * width)
            fields = raw_ref[lead, :, :, lanes].astype(jnp.float32)
            x_ref[lead, cell] = fields.reshape(rows, width).astype(jnp.bfloat16)

    left, right, ahead, _ = neighbours(space_size, shifts, tm_size)
    greet([left, right, *ahead])

    def send(src, dst, lead, slot, peer):
        copy = pltpu.make_async_remote_copy(
            src_ref=src,
            dst_ref=dst,
            send_sem=send_sem.at[lead, slot],
            recv_sem=recv_sem.at[lead, slot],
            device_id=peer,
            device_id_type=MESH,
        )
        copy.start()
        return copy

    parts = ((0, EDGE), (cells - EDGE, EDGE), (EDGE, cells - 2 * EDGE))
    sent = {}
    for lead in (*range(1, leads), 0):
        regroup(lead)
        for slot, (begin, count) in enumerate(parts if lead else ()):
            sent[lead, slot] = send(
                x_ref.at[lead, pl.ds(begin, count)],
                ext_ref.at[lead, pl.ds(begin + EDGE, count)],
                lead,
                slot,
                ahead[lead - 1],
            )
    own = pltpu.make_async_copy(x_ref.at[0], ext_ref.at[0, pl.ds(EDGE, cells)], own_sem)
    own.start()
    edges = [
        send(x_ref.at[0, pl.ds(0, EDGE)], ext_ref.at[0, pl.ds(cells + EDGE, EDGE)], 0, 3, left),
        send(x_ref.at[0, pl.ds(cells - EDGE, EDGE)], ext_ref.at[0, pl.ds(0, EDGE)], 0, 4, right),
    ]
    for slot in (0, 1):
        for lead in range(1, leads):
            sent[lead, slot].wait_recv()
            if slot == 0:
                src, dst, peer = pl.ds(EDGE, EDGE), pl.ds(cells + EDGE, EDGE), left
            else:
                src, dst, peer = pl.ds(cells, EDGE), pl.ds(0, EDGE), right
            edges.append(send(ext_ref.at[lead, src], ext_ref.at[lead, dst], lead, 3 + slot, peer))
    own.wait()
    for lead in range(1, leads):
        sent[lead, 2].wait_recv()
    for copy in edges:
        copy.wait()
    for copy in sent.values():
        copy.wait_send()


def observe_kernel(index_ref, count_ref, ext_ref, op_ref, value_ref, weight_ref, out_ref):
    chunk, width = op_ref.shape[:2]
    leads, _, rows, _ = ext_ref.shape
    step = pl.program_id(0)

    @pl.when(step == 0)
    def _():
        out_ref[...] = jnp.zeros_like(out_ref)

    repeat = 8 // value_ref.shape[0]
    for k in range(chunk):
        block = step * chunk + k
        cell = index_ref[block]
        fields = ext_ref[:, cell].reshape(leads * rows, width)
        operator = op_ref[k]
        images = lax.dot_general(
            fields, operator, (((1,), (1,)), ((), ())), preferred_element_type=jnp.float32
        )
        lanes = slice(k * width, (k + 1) * width)
        observed = value_ref[:, lanes].astype(jnp.float32)
        scaling = weight_ref[:, lanes].astype(jnp.float32)
        slot = block * width + lax.broadcasted_iota(jnp.int32, scaling.shape, 1)
        scaling = jnp.where(slot < count_ref[0], scaling, 0.0)
        observed = jnp.concatenate([observed] * repeat, axis=0)
        scaling = jnp.concatenate([scaling] * repeat, axis=0)
        departures = (images.reshape(-1, 8, width) - observed[None]) * scaling[None]
        misfit = departures.reshape(leads * rows, width).astype(jnp.bfloat16)
        adjoint = jnp.dot(misfit, operator, preferred_element_type=jnp.float32)
        out_ref[:, cell] += adjoint.reshape(leads, rows, width)


def encode(values, coded, scale):
    most = jnp.max(jnp.abs(values), axis=0, keepdims=True)
    most = jnp.maximum(most, 1e-30)
    coded[...] = jnp.round(values * (STEPS / most)).astype(jnp.int32).astype(jnp.int16)
    scale[...] = most * (1.0 / STEPS)


def decode(coded, scale):
    return coded.astype(jnp.int32).astype(jnp.float32) * scale


def return_kernel(
    tm_size,
    space_size,
    shifts,
    adj_ref,
    out_ref,
    below,
    above,
    own_code,
    own_scale,
    part,
    part_scale,
    send_sem,
    recv_sem,
):
    leads, wide, _, width = adj_ref.shape
    cells = wide - 2 * EDGE
    left, right, _, behind = neighbours(space_size, shifts, tm_size)
    greet([left, right, *behind])

    def send(src, dst, lead, slot, peer):
        copy = pltpu.make_async_remote_copy(
            src_ref=src,
            dst_ref=dst,
            send_sem=send_sem.at[lead, slot],
            recv_sem=recv_sem.at[lead, slot],
            device_id=peer,
            device_id_type=MESH,
        )
        copy.start()
        return copy

    low, high, copies = {}, {}, []
    order = [*range(1, leads), 0]
    for lead in order:
        high[lead] = send(adj_ref.at[lead, pl.ds(0, EDGE)], above.at[lead], lead, 0, left)
        low[lead] = send(adj_ref.at[lead, pl.ds(cells + EDGE, EDGE)], below.at[lead], lead, 1, right)

    def hand_back(lead, begin, count, slot):
        span = pl.ds(begin, count)
        for j, (own, other) in enumerate(((own_code, part), (own_scale, part_scale))):
            copies.append(
                send(
                    own.at[lead - 1, span], other.at[lead - 1, span], lead, slot + j, behind[lead - 1]
                )
            )

    for lead in order[:-1]:
        for cell in range(2 * EDGE, cells):
            encode(adj_ref[lead, cell], own_code.at[lead - 1, cell], own_scale.at[lead - 1, cell])
        hand_back(lead, 2 * EDGE, cells - 2 * EDGE, 2)
    for lead in order[:-1]:
        low[lead].wait_recv()
        high[lead].wait_recv()
        for e in range(EDGE):
            encode(
                adj_ref[lead, EDGE + e] + below[lead, e],
                own_code.at[lead - 1, e],
                own_scale.at[lead - 1, e],
            )
            encode(
                adj_ref[lead, cells + e] + above[lead, e],
                own_code.at[lead - 1, EDGE + e],
                own_scale.at[lead - 1, EDGE + e],
            )
        hand_back(lead, 0, 2 * EDGE, 4)
    low[0].wait_recv()
    high[0].wait_recv()
    for copy in copies:
        copy.wait_recv()
    for cell in range(cells):
        total = adj_ref[0, cell + EDGE]
        place = cell + EDGE
        if cell < EDGE:
            total = total + below[0, cell]
            place = cell
        if cell >= cells - EDGE:
            total = total + above[0, cell - (cells - EDGE)]
            place = cell - (cells - EDGE) + EDGE
        for lead in range(1, leads):
            total = total + decode(part[lead - 1, place], part_scale[lead - 1, place])
        out_ref[:, cell * width : (cell + 1) * width] = total
    for copy in (*copies, *low.values(), *high.values()):
        copy.wait_send()


def body(mesh, hindcast_archive, op_blocks, block_index, obs_values, obs_weights, obs_counts):
    tm_size, space_size = mesh.shape["tm"], mesh.shape["space"]
    _, leads, members, layers, points = hindcast_archive.shape
    _, blocks, width, _ = op_blocks.shape
    rows, cells = members * layers, points // width
    wide = cells + 2 * EDGE
    shifts = [lead * tm_size // leads for lead in range(1, leads)]
    extended = pl.pallas_call(
        functools.partial(gather_kernel, tm_size, space_size, shifts),
        out_shape=jax.ShapeDtypeStruct((leads, wide, rows, width), jnp.bfloat16),
        in_specs=[VMEM],
        out_specs=ANY,
        scratch_shapes=[
            pltpu.VMEM((leads, cells, rows, width), jnp.bfloat16),
            pltpu.SemaphoreType.DMA,
            pltpu.SemaphoreType.DMA((leads, 5)),
            pltpu.SemaphoreType.DMA((leads, 5)),
        ],
        compiler_params=pltpu.CompilerParams(collective_id=0, has_side_effects=True),
    )(hindcast_archive[0])
    chunk = 32 if blocks % 32 == 0 else 1
    adjoint = pl.pallas_call(
        observe_kernel,
        out_shape=jax.ShapeDtypeStruct((leads, wide, rows, width), jnp.float32),
        grid_spec=pltpu.PrefetchScalarGridSpec(
            num_scalar_prefetch=2,
            grid=(blocks // chunk,),
            in_specs=[
                pl.BlockSpec((leads, wide, rows, width), lambda g, *_: (0, 0, 0, 0)),
                pl.BlockSpec((chunk, width, width), lambda g, *_: (g, 0, 0)),
                pl.BlockSpec((layers, chunk * width), lambda g, *_: (0, g)),
                pl.BlockSpec((layers, chunk * width), lambda g, *_: (0, g)),
            ],
            out_specs=pl.BlockSpec((leads, wide, rows, width), lambda g, *_: (0, 0, 0, 0)),
        ),
        compiler_params=pltpu.CompilerParams(vmem_limit_bytes=63 << 20),
    )(
        block_index[0],
        obs_counts[0],
        extended,
        op_blocks[0],
        obs_values[0],
        obs_weights[0],
    )
    gradient = pl.pallas_call(
        functools.partial(return_kernel, tm_size, space_size, shifts),
        out_shape=jax.ShapeDtypeStruct((rows, points), jnp.float32),
        in_specs=[VMEM],
        out_specs=VMEM,
        scratch_shapes=[
            pltpu.VMEM((leads, EDGE, rows, width), jnp.float32),
            pltpu.VMEM((leads, EDGE, rows, width), jnp.float32),
            pltpu.VMEM((leads - 1, cells, rows, width), jnp.int16),
            pltpu.VMEM((leads - 1, cells, 1, width), jnp.float32),
            pltpu.VMEM((leads - 1, cells, rows, width), jnp.int16),
            pltpu.VMEM((leads - 1, cells, 1, width), jnp.float32),
            pltpu.SemaphoreType.DMA((leads, 6)),
            pltpu.SemaphoreType.DMA((leads, 6)),
        ],
        compiler_params=pltpu.CompilerParams(
            collective_id=1, has_side_effects=True, vmem_limit_bytes=32 << 20
        ),
    )(adjoint)
    return gradient.reshape(1, members, layers, points)


def solution(mesh):
    in_specs = (
        P("tm", None, None, None, "space"),
        P("tm", "space", None, None),
        P("tm", "space"),
        P("tm", None, "space"),
        P("tm", None, "space"),
        P("tm", "space"),
    )
    out_specs = P("tm", None, None, "space")
    return jax.shard_map(
        functools.partial(body, mesh),
        mesh=mesh,
        in_specs=in_specs,
        out_specs=out_specs,
        check_vma=False,
    )
```
